32 devices in a mesh: ctx: 8 (over z, y), head: 4 (over x, core).
Axes of the slice: x: 2, y: 2, z: 4, core: 2. Of those that a mesh axis runs over, the one named last changes fastest.
Arguments:
- prompt_hidden: bfloat16 [4, 4096, 5120], P(None, 'ctx', 'head'), may hold values from -6 to 6
- prompt_lengths: int32 [4], replicated, may hold values from 2048 to 4096, as said below
- group_prompt: int32 [8], replicated, may hold values from 0 to 3, as said below
- sample_hidden: bfloat16 [8, 4, 16, 5120], P('ctx'), may hold values from -6 to 6
- norm_gain: float32 [5120], replicated, may hold values from 0.1 to 1.9
- q_gain: float32 [128], replicated, may hold values from 0.5 to 6
- k_gain: float32 [128], replicated, may hold values from 0.5 to 6
- w_q: bfloat16 [5120, 8192], P('ctx', 'head'), may hold values from -0.078125 to 0.078125
- w_kv: bfloat16 [5120, 2, 1024], P(None, None, 'head'), may hold values from -0.078125 to 0.078125
- w_o: bfloat16 [8192, 5120], P('head', 'ctx'), may hold values from -0.375 to 0.375
Outputs:
- decoded: bfloat16 [8, 4, 16, 5120], P('ctx', None, None, 'head')
- kv_cache: bfloat16 [8, 4096, 2, 1024], P('ctx', None, None, 'head')
The draws below stay inside these ranges and needn't reach their ends.
Inputs may be any that keep to these rules, and one draw needn't show every extreme that they name: `prompt_lengths`: one prompt has exactly 4096 live positions and another exactly 2048. `group_prompt`: each prompt is sampled by exactly 2 groups.
All inputs are finite; a program needn't handle non-finite values.
Results may differ from the reference program's by a relative error of at most 0.007.
The reference program's roundings to bfloat16 on the way count: a program that leaves them out, or rounds other values in their place, can miss the bound.
Values may be sent and summed in bfloat16 or wider, within the bound.
A program may use at most 256 MiB of HBM per device.

```python
import jax
import jax.numpy as jnp
from jax import lax

D = 5120
HEADS = 64
KV_HEADS = 8
HEAD_DIM = 128
PROMPTS = 4
SAMPLES = 16
STEPS = 4
GROUPS = 8
LMAX = 4096


def gain_values(key, lowest, highest):
    uniform_part = jax.random.uniform(key, (HEAD_DIM,), jnp.float32)
    return jnp.exp(jnp.log(lowest) + uniform_part * (jnp.log(highest) - jnp.log(lowest)))


def draw_q_gain(key, part):
    key = jax.random.fold_in(key, 11)
    return gain_values(key, 0.5, 2.5)


def draw_k_gain(key, part):
    key = jax.random.fold_in(key, 23)
    return gain_values(key, 0.5, 2.5)


def draw_prompt_lengths(key, part):
    key = jax.random.fold_in(key, 5)
    first_key, second_key, third_key = jax.random.split(key, 3)
    lengths = jax.random.randint(first_key, (PROMPTS,), LMAX // 2, LMAX + 1)
    longest = jax.random.randint(second_key, (), 0, PROMPTS)
    shortest = (longest + jax.random.randint(third_key, (), 1, PROMPTS)) % PROMPTS
    lengths = lengths.at[longest].set(LMAX).at[shortest].set(LMAX // 2)
    return lengths.astype(jnp.int32)


def draw_group_prompt(key, part):
    key = jax.random.fold_in(key, 37)
    table = (jnp.arange(GROUPS, dtype=jnp.int32) % PROMPTS).astype(jnp.int32)
    return jax.random.permutation(key, table).astype(jnp.int32)


def with_spikes(drawn, rng, source, target, blocks, factor):
    owner, partner = [(jnp.arange(drawn.shape[dim]) // (drawn.shape[dim] // blocks)).reshape([-1 if axis == dim else 1 for axis in range(drawn.ndim)]) for dim in (source, target)]
    chosen = jax.random.permutation(rng, blocks)[partner]
    strong = (owner == chosen) | (owner == (partner + blocks // 2) % blocks)
    return jnp.where(strong, factor * drawn, drawn)


def shard_levels(stream_key, dims, pieces, low, top_value):
    level, own = 1.0, jax.random.fold_in(stream_key, 6)
    for dim, shards_of in pieces:
        heights = jnp.exp(jax.random.uniform(jax.random.fold_in(own, dim), (shards_of,), jnp.float32, low / len(pieces), top_value / len(pieces)))
        level = level * jnp.repeat(heights, dims[dim] // shards_of).reshape([-1 if axis == dim else 1 for axis in range(len(dims))])
    return level


def gaussian(stream_key, shape, width, reach, pieces=(), kind=jnp.bfloat16):
    array = jax.random.normal(stream_key, shape, jnp.float32) * width
    if len(pieces) > 0:
        array = shard_levels(stream_key, shape, pieces, -0.22, 0.18) * array
    return jnp.clip(array, min=-reach, max=reach).astype(kind)


def gaussian_with(own_key, shape, spread, limit, shards, heavy, held_as=jnp.bfloat16):
    entries = spread * jax.random.normal(own_key, shape, jnp.float32)
    if shards:
        entries = entries * shard_levels(own_key, shape, shards, -0.22, 0.18)
    return jnp.clip(with_spikes(entries, jax.random.fold_in(own_key, 3), *heavy), -limit, limit).astype(held_as)


def setup_inputs(seed: int = 0) -> dict:
    key_of = jax.random.split(jax.random.key(seed), 11)
    return {
        "prompt_hidden": gaussian(key_of[0], (PROMPTS, LMAX, D), 1.0, 6.0, ((1, 8), (2, 4))),
        "prompt_lengths": draw_prompt_lengths(jax.random.fold_in(key_of[10], 71), 0),
        "group_prompt": draw_group_prompt(jax.random.fold_in(key_of[10], 71), 0),
        "sample_hidden": gaussian(key_of[3], (GROUPS, STEPS, SAMPLES, D), 1.0, 6.0, ((0, 8),)),
        "norm_gain": jnp.clip(1.0 + 0.18 * jax.random.normal(key_of[4], (D,), jnp.float32), 0.1, 1.9),
        "q_gain": draw_q_gain(jax.random.fold_in(key_of[10], 71), 0),
        "k_gain": draw_k_gain(jax.random.fold_in(key_of[10], 71), 0),
        "w_q": gaussian(key_of[7], (D, HEADS * HEAD_DIM), D ** -0.5, 0.078125, ((0, 8), (1, 4))),
        "w_kv": gaussian(key_of[8], (D, 2, KV_HEADS * HEAD_DIM), D ** -0.5, 0.078125, ((2, 4),)),
        "w_o": gaussian_with(key_of[9], (HEADS * HEAD_DIM, D), (HEADS * HEAD_DIM // 16) ** -0.5, 0.375, ((0, 4), (1, 8)), (0, 1, 8, 2.0)),
    }


EPS = 1e-06
THETA = 1000000.0

def rotary(vector, position):
    half_size = vector.shape[-1] // 2
    frequency = THETA ** (-jnp.arange(half_size, dtype=jnp.float32) * 2.0 / vector.shape[-1])
    angle = position[..., None] * frequency
    cosine = jnp.cos(angle)
    sine = jnp.sin(angle)
    first = vector[..., :half_size]
    second = vector[..., half_size:]
    return jnp.concatenate([first * cosine - second * sine, second * cosine + first * sine], -1)

def head_norm(vector, gain):
    return vector * lax.rsqrt(lax.optimization_barrier(jnp.mean(vector * vector, -1, keepdims=True)) + EPS) * gain

def prefill_prompt(hidden, norm_gain, k_gain, w_kv):
    wide = hidden.astype(jnp.float32)
    inverse = lax.rsqrt(lax.optimization_barrier(jnp.mean(wide * wide, -1)) + EPS)[:, None]
    scaled = (wide * norm_gain).astype(jnp.bfloat16)
    raw = jnp.dot(scaled, w_kv.reshape(D, 2 * KV_HEADS * HEAD_DIM), preferred_element_type=jnp.float32) * inverse
    raw = raw.reshape(LMAX, 2, KV_HEADS, HEAD_DIM)
    positions = jnp.arange(LMAX).astype(jnp.float32)
    keys = rotary(head_norm(raw[:, 0], k_gain), positions[:, None])
    both = jnp.stack([keys, raw[:, 1]], 1).astype(jnp.bfloat16)
    return both.reshape(LMAX, 2, KV_HEADS * HEAD_DIM)

def attend(queries, prefix_keys, prefix_values, new_keys, new_values, length, samples):
    total_rows = queries.shape[0]
    query_wide = queries.astype(jnp.float32)
    prefix_scores = jnp.einsum('rkgd,lkd->kgrl', query_wide, prefix_keys.astype(jnp.float32))
    suffix_scores = jnp.einsum('rkgd,ukd->kgru', query_wide, new_keys.astype(jnp.float32))
    live = jnp.arange(prefix_keys.shape[0]) < length
    prefix_scores = jnp.where(live, prefix_scores, -1e+30)
    row_index = jnp.arange(total_rows)
    same_sample = row_index[:, None] % samples == row_index[None, :] % samples
    earlier = row_index[None, :] // samples <= row_index[:, None] // samples
    suffix_scores = jnp.where(same_sample & earlier, suffix_scores, -1e+30)
    top = jnp.maximum(lax.optimization_barrier(jnp.max(prefix_scores, -1, keepdims=True)), lax.optimization_barrier(jnp.max(suffix_scores, -1, keepdims=True)))
    prefix_exp = jnp.exp(prefix_scores - top)
    suffix_exp = jnp.exp(suffix_scores - top)
    total = lax.optimization_barrier(jnp.sum(prefix_exp, -1, keepdims=True)) + lax.optimization_barrier(jnp.sum(suffix_exp, -1, keepdims=True))
    prefix_weight = (prefix_exp / total).astype(jnp.bfloat16)
    suffix_weight = (suffix_exp / total).astype(jnp.bfloat16)
    result = jnp.einsum('kgrl,lkd->rkgd', prefix_weight.astype(jnp.float32), prefix_values.astype(jnp.float32))
    result = result + jnp.einsum('kgru,ukd->rkgd', suffix_weight.astype(jnp.float32), new_values.astype(jnp.float32))
    return result.reshape(total_rows, -1).astype(jnp.bfloat16)

def decode_group(tokens, cache, length, norm_gain, q_gain, k_gain, w_q, w_kv, w_o):
    flat = tokens.reshape(STEPS * SAMPLES, D)
    wide = flat.astype(jnp.float32)
    inverse = lax.rsqrt(lax.optimization_barrier(jnp.mean(wide * wide, -1)) + EPS)[:, None]
    scaled = (wide * norm_gain).astype(jnp.bfloat16)
    queries = jnp.dot(scaled, w_q, preferred_element_type=jnp.float32) * inverse
    fresh = jnp.dot(scaled, w_kv.reshape(D, 2 * KV_HEADS * HEAD_DIM), preferred_element_type=jnp.float32) * inverse
    fresh = fresh.reshape(STEPS * SAMPLES, 2, KV_HEADS, HEAD_DIM)
    row_position = jnp.repeat(length + jnp.arange(STEPS, dtype=jnp.int32), SAMPLES).astype(jnp.float32)
    queries = rotary(head_norm(queries.reshape(STEPS * SAMPLES, HEADS, HEAD_DIM), q_gain), row_position[:, None])
    queries = (queries * HEAD_DIM ** (-0.5)).astype(jnp.bfloat16)
    queries = queries.reshape(STEPS * SAMPLES, KV_HEADS, HEADS // KV_HEADS, HEAD_DIM)
    new_keys = rotary(head_norm(fresh[:, 0], k_gain), row_position[:, None]).astype(jnp.bfloat16)
    new_values = fresh[:, 1].astype(jnp.bfloat16)
    prefix_keys = cache[:, 0].reshape(LMAX, KV_HEADS, HEAD_DIM)
    prefix_values = cache[:, 1].reshape(LMAX, KV_HEADS, HEAD_DIM)
    attended = attend(queries, prefix_keys, prefix_values, new_keys, new_values, length, SAMPLES)
    result = wide + jnp.dot(attended, w_o, preferred_element_type=jnp.float32)
    return result.astype(jnp.bfloat16).reshape(STEPS, SAMPLES, D)

def reference(prompt_hidden, prompt_lengths, group_prompt, sample_hidden, norm_gain, q_gain, k_gain, w_q, w_kv, w_o):
    caches = lax.map(lambda hidden: prefill_prompt(hidden, norm_gain, k_gain, w_kv), prompt_hidden)
    regrouped = jnp.take(caches, group_prompt, axis=0)
    lengths = jnp.take(prompt_lengths, group_prompt)
    decoded = lax.map(lambda items: decode_group(items[0], items[1], items[2], norm_gain, q_gain, k_gain, w_q, w_kv, w_o), (sample_hidden, regrouped, lengths))
    return (decoded, regrouped)
```

```python
import jax
import jax.numpy as jnp
from jax import lax
from jax.sharding import PartitionSpec as P

EPS = 1e-06
THETA = 1000000.0
CHUNKS = 2


def rotary(vector, position):
    half_size = vector.shape[-1] // 2
    frequency = THETA ** (-jnp.arange(half_size, dtype=jnp.float32) * 2.0 / vector.shape[-1])
    angle = position[..., None] * frequency
    cosine = jnp.cos(angle)
    sine = jnp.sin(angle)
    first = vector[..., :half_size]
    second = vector[..., half_size:]
    return jnp.concatenate([first * cosine - second * sine, second * cosine + first * sine], -1)


def head_norm(vector, gain):
    return vector * lax.rsqrt(jnp.mean(vector * vector, -1, keepdims=True) + EPS) * gain


def attend(queries, prefix_keys, prefix_values, new_keys, new_values, length, samples):
    total_rows = queries.shape[0]
    prefix_scores = jnp.einsum(
        "rkgd,lkd->kgrl", queries, prefix_keys, preferred_element_type=jnp.float32
    )
    suffix_scores = jnp.einsum(
        "rkgd,ukd->kgru", queries, new_keys, preferred_element_type=jnp.float32
    )
    live = jnp.arange(prefix_keys.shape[0]) < length
    prefix_scores = jnp.where(live, prefix_scores, -1e30)
    row_index = jnp.arange(total_rows)
    same_sample = row_index[:, None] % samples == row_index[None, :] % samples
    earlier = row_index[None, :] // samples <= row_index[:, None] // samples
    suffix_scores = jnp.where(same_sample & earlier, suffix_scores, -1e30)
    top = jnp.maximum(
        jnp.max(prefix_scores, -1, keepdims=True), jnp.max(suffix_scores, -1, keepdims=True)
    )
    prefix_exp = jnp.exp(prefix_scores - top)
    suffix_exp = jnp.exp(suffix_scores - top)
    total = jnp.sum(prefix_exp, -1, keepdims=True) + jnp.sum(suffix_exp, -1, keepdims=True)
    prefix_weight = (prefix_exp / total).astype(jnp.bfloat16)
    suffix_weight = (suffix_exp / total).astype(jnp.bfloat16)
    result = jnp.einsum(
        "kgrl,lkd->rkgd", prefix_weight, prefix_values, preferred_element_type=jnp.float32
    )
    result = result + jnp.einsum(
        "kgru,ukd->rkgd", suffix_weight, new_values, preferred_element_type=jnp.float32
    )
    return result.reshape(total_rows, -1).astype(jnp.bfloat16)


def local(
    prompt_hidden,
    prompt_lengths,
    group_prompt,
    sample_hidden,
    norm_gain,
    q_gain,
    k_gain,
    w_q,
    w_kv,
    w_o,
):
    prompts, slab, part_width = prompt_hidden.shape
    model_width = norm_gain.shape[0]
    head_dim = q_gain.shape[0]
    kv_width = w_kv.shape[2]
    kv_local = kv_width // head_dim
    q_width = w_q.shape[1]
    q_local = q_width // head_dim
    group_size = q_local // kv_local
    ctx_index = lax.axis_index("ctx")
    ctx_size = lax.axis_size("ctx")
    flat_weights = w_kv.reshape(model_width, 2 * kv_width)
    steps = sample_hidden.shape[1]
    samples = sample_hidden.shape[2]
    token_rows = steps * samples
    wide = sample_hidden.reshape(token_rows, model_width).astype(jnp.float32)
    token_inverse = lax.rsqrt(jnp.mean(wide * wide, -1) + EPS)[:, None]
    token_scaled = (wide * norm_gain).astype(jnp.bfloat16)
    row_depth = w_q.shape[0]
    by_feature = token_scaled.reshape(token_rows, ctx_size, row_depth).transpose(1, 0, 2)
    all_tokens = lax.all_to_all(by_feature, "ctx", split_axis=0, concat_axis=0, tiled=True)
    query_part = jnp.dot(
        all_tokens.reshape(ctx_size * token_rows, row_depth), w_q, preferred_element_type=jnp.float32
    ).reshape(ctx_size, token_rows, q_width)
    query_part = lax.all_to_all(query_part, "ctx", split_axis=0, concat_axis=0, tiled=True)
    queries = jnp.sum(query_part, 0) * token_inverse

    chunk_rows = slab // CHUNKS
    cache_chunks = []
    for chunk in range(CHUNKS):
        hidden = lax.slice_in_dim(prompt_hidden, chunk * chunk_rows, (chunk + 1) * chunk_rows, axis=1)
        piece = lax.all_gather(hidden, "head", axis=2, tiled=True)
        wide_piece = piece.astype(jnp.float32).reshape(prompts * chunk_rows, model_width)
        scaled_piece = (wide_piece * norm_gain).astype(jnp.bfloat16)
        running_sum = jnp.dot(scaled_piece, flat_weights, preferred_element_type=jnp.float32)
        squares = jnp.sum(wide_piece * wide_piece, -1)
        prefill_inverse = lax.rsqrt(squares / model_width + EPS)[:, None]
        raw = (running_sum * prefill_inverse).reshape(prompts, chunk_rows, 2, kv_local, head_dim)
        positions = (
            ctx_index * slab + chunk * chunk_rows + jnp.arange(chunk_rows, dtype=jnp.int32)
        ).astype(jnp.float32)
        prompt_keys = rotary(head_norm(raw[:, :, 0], k_gain), positions[None, :, None])
        cache_local = jnp.stack([prompt_keys, raw[:, :, 1]], 2).astype(jnp.bfloat16)
        cache_local = cache_local.reshape(prompts, chunk_rows, 2, kv_width)
        ordered = jnp.take(cache_local, group_prompt, axis=0)
        cache_chunks.append(
            lax.all_to_all(ordered, "ctx", split_axis=0, concat_axis=0, tiled=True)
        )
    kv_cache = jnp.stack(cache_chunks, 1).reshape(1, ctx_size * slab, 2, kv_width)
    length = jnp.take(prompt_lengths, jnp.take(group_prompt, ctx_index))
    fresh = jnp.dot(token_scaled, flat_weights, preferred_element_type=jnp.float32) * token_inverse
    fresh = fresh.reshape(token_rows, 2, kv_local, head_dim)
    row_position = jnp.repeat(length + jnp.arange(steps, dtype=jnp.int32), samples).astype(
        jnp.float32
    )
    queries = rotary(
        head_norm(queries.reshape(token_rows, q_local, head_dim), q_gain), row_position[:, None]
    )
    queries = (queries * head_dim ** (-0.5)).astype(jnp.bfloat16)
    queries = queries.reshape(token_rows, kv_local, group_size, head_dim)
    new_keys = rotary(head_norm(fresh[:, 0], k_gain), row_position[:, None]).astype(jnp.bfloat16)
    new_values = fresh[:, 1].astype(jnp.bfloat16)
    prefix_keys = kv_cache[0, :, 0].reshape(-1, kv_local, head_dim)
    prefix_values = kv_cache[0, :, 1].reshape(-1, kv_local, head_dim)
    attended = attend(queries, prefix_keys, prefix_values, new_keys, new_values, length, samples)
    all_attended = lax.all_gather(attended, "ctx", axis=0, tiled=True)
    partial_out = jnp.dot(all_attended, w_o, preferred_element_type=jnp.float32)
    partial_out = lax.all_to_all(
        partial_out.reshape(ctx_size, token_rows, w_o.shape[1]),
        "ctx", split_axis=0, concat_axis=0, tiled=True,
    )
    partial_out = partial_out.transpose(1, 0, 2).reshape(token_rows, model_width)
    summed = lax.psum_scatter(partial_out, "head", scatter_dimension=1, tiled=True)
    out_width = summed.shape[1]
    residual = lax.dynamic_slice_in_dim(wide, lax.axis_index("head") * out_width, out_width, 1)
    decoded = (residual + summed).astype(jnp.bfloat16).reshape(1, steps, samples, out_width)
    return (decoded, kv_cache)


def solution(mesh):
    return jax.shard_map(
        local,
        mesh=mesh,
        in_specs=(
            P(None, "ctx", "head"),
            P(),
            P(),
            P("ctx", None, None, None),
            P(),
            P(),
            P(),
            P("ctx", "head"),
            P(None, None, "head"),
            P("head", "ctx"),
        ),
        out_specs=(P("ctx", None, None, "head"), P("ctx", None, None, "head")),
        check_vma=False,
    )
```

```python
import functools

import jax
import jax.numpy as jnp
from jax import lax
from jax.experimental import pallas as pl
from jax.experimental.pallas import tpu as pltpu
from jax.sharding import PartitionSpec as P

EPS = 1e-06
THETA = 1000000.0
CHUNKS = 2


def rotary(vector, position):
    half_size = vector.shape[-1] // 2
    frequency = THETA ** (-jnp.arange(half_size, dtype=jnp.float32) * 2.0 / vector.shape[-1])
    angle = position[..., None] * frequency
    cosine = jnp.cos(angle)
    sine = jnp.sin(angle)
    first = vector[..., :half_size]
    second = vector[..., half_size:]
    return jnp.concatenate([first * cosine - second * sine, second * cosine + first * sine], -1)


def head_norm(vector, gain):
    return vector * lax.rsqrt(jnp.mean(vector * vector, -1, keepdims=True) + EPS) * gain


def attend(queries, prefix_keys, prefix_values, new_keys, new_values, length, samples):
    total_rows = queries.shape[0]
    prefix_scores = jnp.einsum(
        "rkgd,lkd->kgrl", queries, prefix_keys, preferred_element_type=jnp.float32
    )
    suffix_scores = jnp.einsum(
        "rkgd,ukd->kgru", queries, new_keys, preferred_element_type=jnp.float32
    )
    live = jnp.arange(prefix_keys.shape[0]) < length
    prefix_scores = jnp.where(live, prefix_scores, -1e30)
    row_index = jnp.arange(total_rows)
    same_sample = row_index[:, None] % samples == row_index[None, :] % samples
    earlier = row_index[None, :] // samples <= row_index[:, None] // samples
    suffix_scores = jnp.where(same_sample & earlier, suffix_scores, -1e30)
    top = jnp.maximum(
        jnp.max(prefix_scores, -1, keepdims=True), jnp.max(suffix_scores, -1, keepdims=True)
    )
    prefix_exp = jnp.exp(prefix_scores - top)
    suffix_exp = jnp.exp(suffix_scores - top)
    total = jnp.sum(prefix_exp, -1, keepdims=True) + jnp.sum(suffix_exp, -1, keepdims=True)
    prefix_weight = (prefix_exp / total).astype(jnp.bfloat16)
    suffix_weight = (suffix_exp / total).astype(jnp.bfloat16)
    result = jnp.einsum(
        "kgrl,lkd->rkgd", prefix_weight, prefix_values, preferred_element_type=jnp.float32
    )
    result = result + jnp.einsum(
        "kgru,ukd->rkgd", suffix_weight, new_values, preferred_element_type=jnp.float32
    )
    return result.reshape(total_rows, -1).astype(jnp.bfloat16)


def project_kernel(
    ctx_size, head_size, attended_ref, w_ref, out_ref,
    gathered, partial, landed, gather_send, gather_recv, part_send, part_recv, own_sem,
):
    ctx = lax.axis_index("ctx")
    head = lax.axis_index("head")
    per = ctx_size // head_size
    owner = ctx // per
    rank = ctx % per
    is_owner = owner == head
    mesh_id = pl.DeviceIdType.MESH

    barrier = pltpu.get_barrier_semaphore()
    for k in range(1, ctx_size):
        source = lax.rem(ctx - k + ctx_size, ctx_size)
        pl.semaphore_signal(barrier, inc=1, device_id=(source, head), device_id_type=mesh_id)
    for h in range(head_size):
        for r in range(per):
            source = head * per + r

            @pl.when(jnp.logical_or(source != ctx, h != head))
            def _():
                pl.semaphore_signal(barrier, inc=1, device_id=(source, h), device_id_type=mesh_id)

    @pl.when(is_owner)
    def _():
        pl.semaphore_wait(barrier, 2 * ctx_size - 2)

    @pl.when(jnp.logical_not(is_owner))
    def _():
        pl.semaphore_wait(barrier, 2 * ctx_size - 1)

    def gather_copy(k):
        target = lax.rem(ctx + k, ctx_size)
        return pltpu.make_async_remote_copy(
            src_ref=attended_ref, dst_ref=gathered.at[k],
            send_sem=gather_send.at[k], recv_sem=gather_recv.at[k],
            device_id=(target, head), device_id_type=mesh_id,
        )

    def part_copy(k):
        target = lax.rem(ctx - k + ctx_size, ctx_size)
        slot = head * per + rank
        return pltpu.make_async_remote_copy(
            src_ref=partial.at[k], dst_ref=landed.at[slot],
            send_sem=part_send.at[k], recv_sem=part_recv.at[slot],
            device_id=(target, owner), device_id_type=mesh_id,
        )

    def own_copy():
        return pltpu.make_async_copy(partial.at[0], landed.at[head * per + rank], own_sem)

    for k in range(1, ctx_size):
        gather_copy(k).start()
    gathered[0] = attended_ref[...]
    rows, depth = attended_ref.shape
    width = w_ref.shape[1]
    half = ctx_size // 2
    for part in range(2):
        first = part * half
        for k in range(max(first, 1), first + half):
            gather_copy(k).wait_recv()
        block = gathered[first : first + half].reshape(half * rows, depth)
        product = jnp.dot(block, w_ref[...], preferred_element_type=jnp.float32)
        partial[first : first + half] = product.reshape(half, rows, width)
        for k in range(first, first + half):
            if k:
                part_copy(k).start()
            else:

                @pl.when(is_owner)
                def _():
                    own_copy().start()

                @pl.when(jnp.logical_not(is_owner))
                def _():
                    part_copy(0).start()

    for k in range(1, ctx_size):
        gather_copy(k).wait_send()
    for r in range(per):
        source = head * per + r
        for h in range(head_size):
            mine = jnp.logical_and(source == ctx, h == head)
            slot = h * per + r

            @pl.when(mine)
            def _():
                own_copy().wait()

            @pl.when(jnp.logical_not(mine))
            def _():
                pltpu.make_async_remote_copy(
                    src_ref=partial.at[0], dst_ref=landed.at[slot],
                    send_sem=part_send.at[0], recv_sem=part_recv.at[slot],
                    device_id=(source, h), device_id_type=mesh_id,
                ).wait_recv()

        total = landed[r]
        for h in range(1, head_size):
            total = total + landed[h * per + r]
        out_ref[:, r * width : (r + 1) * width] = total
    for k in range(ctx_size):
        if k:
            part_copy(k).wait_send()
        else:

            @pl.when(jnp.logical_not(is_owner))
            def _():
                part_copy(0).wait_send()


def project(attended, w_o):
    ctx_size = lax.axis_size("ctx")
    head_size = lax.axis_size("head")
    per = ctx_size // head_size
    rows, depth = attended.shape
    width = w_o.shape[1]
    return pl.pallas_call(
        functools.partial(project_kernel, ctx_size, head_size),
        out_shape=jax.ShapeDtypeStruct((rows, per * width), jnp.float32),
        in_specs=[pl.BlockSpec(memory_space=pltpu.VMEM)] * 2,
        out_specs=pl.BlockSpec(memory_space=pltpu.VMEM),
        scratch_shapes=[
            pltpu.VMEM((ctx_size, rows, depth), jnp.bfloat16),
            pltpu.VMEM((ctx_size, rows, width), jnp.float32),
            pltpu.VMEM((head_size * per, rows, width), jnp.float32),
            pltpu.SemaphoreType.DMA((ctx_size,)),
            pltpu.SemaphoreType.DMA((ctx_size,)),
            pltpu.SemaphoreType.DMA((ctx_size,)),
            pltpu.SemaphoreType.DMA((head_size * per,)),
            pltpu.SemaphoreType.DMA,
        ],
        compiler_params=pltpu.CompilerParams(
            collective_id=0, has_side_effects=True, vmem_limit_bytes=32 * 1024 * 1024
        ),
        cost_estimate=pl.CostEstimate(
            flops=2 * ctx_size * rows * depth * width,
            bytes_accessed=2 * (depth * width + ctx_size * rows * depth),
            transcendentals=0,
        ),
    )(attended, w_o)


def local(
    prompt_hidden,
    prompt_lengths,
    group_prompt,
    sample_hidden,
    norm_gain,
    q_gain,
    k_gain,
    w_q,
    w_kv,
    w_o,
):
    prompts, slab, part_width = prompt_hidden.shape
    model_width = norm_gain.shape[0]
    head_dim = q_gain.shape[0]
    kv_width = w_kv.shape[2]
    kv_local = kv_width // head_dim
    q_width = w_q.shape[1]
    q_local = q_width // head_dim
    group_size = q_local // kv_local
    ctx_index = lax.axis_index("ctx")
    ctx_size = lax.axis_size("ctx")
    flat_weights = w_kv.reshape(model_width, 2 * kv_width)
    steps = sample_hidden.shape[1]
    samples = sample_hidden.shape[2]
    token_rows = steps * samples
    wide = sample_hidden.reshape(token_rows, model_width).astype(jnp.float32)
    token_inverse = lax.rsqrt(jnp.mean(wide * wide, -1) + EPS)[:, None]
    token_scaled = (wide * norm_gain).astype(jnp.bfloat16)
    row_depth = w_q.shape[0]
    by_feature = token_scaled.reshape(token_rows, ctx_size, row_depth).transpose(1, 0, 2)
    all_tokens = lax.all_to_all(by_feature, "ctx", split_axis=0, concat_axis=0, tiled=True)
    query_part = jnp.dot(
        all_tokens.reshape(ctx_size * token_rows, row_depth), w_q, preferred_element_type=jnp.float32
    ).reshape(ctx_size, token_rows, q_width)
    query_part = lax.all_to_all(query_part, "ctx", split_axis=0, concat_axis=0, tiled=True)
    queries = jnp.sum(query_part, 0) * token_inverse

    chunk_rows = slab // CHUNKS
    exchange = functools.partial(
        lax.all_to_all, axis_name="ctx", split_axis=0, concat_axis=0, tiled=True
    )
    cache_chunks = []
    for chunk in range(CHUNKS):
        hidden = lax.slice_in_dim(prompt_hidden, chunk * chunk_rows, (chunk + 1) * chunk_rows, axis=1)
        piece = lax.all_gather(hidden, "head", axis=2, tiled=True)
        if cache_chunks:
            piece, ordered = lax.optimization_barrier((piece, ordered))
            cache_chunks[-1] = exchange(ordered)
        wide_piece = piece.astype(jnp.float32).reshape(prompts * chunk_rows, model_width)
        scaled_piece = (wide_piece * norm_gain).astype(jnp.bfloat16)
        running_sum = jnp.dot(scaled_piece, flat_weights, preferred_element_type=jnp.float32)
        squares = jnp.sum(wide_piece * wide_piece, -1)
        prefill_inverse = lax.rsqrt(squares / model_width + EPS)[:, None]
        raw = (running_sum * prefill_inverse).reshape(prompts, chunk_rows, 2, kv_local, head_dim)
        positions = (
            ctx_index * slab + chunk * chunk_rows + jnp.arange(chunk_rows, dtype=jnp.int32)
        ).astype(jnp.float32)
        prompt_keys = rotary(head_norm(raw[:, :, 0], k_gain), positions[None, :, None])
        cache_local = jnp.stack([prompt_keys, raw[:, :, 1]], 2).astype(jnp.bfloat16)
        cache_local = cache_local.reshape(prompts, chunk_rows, 2, kv_width)
        ordered = jnp.take(cache_local, group_prompt, axis=0)
        cache_chunks.append(None)
    cache_chunks[-1] = exchange(ordered)
    kv_cache = jnp.stack(cache_chunks, 1).reshape(1, ctx_size * slab, 2, kv_width)
    length = jnp.take(prompt_lengths, jnp.take(group_prompt, ctx_index))
    fresh = jnp.dot(token_scaled, flat_weights, preferred_element_type=jnp.float32) * token_inverse
    fresh = fresh.reshape(token_rows, 2, kv_local, head_dim)
    row_position = jnp.repeat(length + jnp.arange(steps, dtype=jnp.int32), samples).astype(
        jnp.float32
    )
    queries = rotary(
        head_norm(queries.reshape(token_rows, q_local, head_dim), q_gain), row_position[:, None]
    )
    queries = (queries * head_dim ** (-0.5)).astype(jnp.bfloat16)
    queries = queries.reshape(token_rows, kv_local, group_size, head_dim)
    new_keys = rotary(head_norm(fresh[:, 0], k_gain), row_position[:, None]).astype(jnp.bfloat16)
    new_values = fresh[:, 1].astype(jnp.bfloat16)
    prefix_keys = kv_cache[0, :, 0].reshape(-1, kv_local, head_dim)
    prefix_values = kv_cache[0, :, 1].reshape(-1, kv_local, head_dim)
    attended = attend(queries, prefix_keys, prefix_values, new_keys, new_values, length, samples)
    summed = project(attended, w_o)
    out_width = summed.shape[1]
    residual = lax.dynamic_slice_in_dim(wide, lax.axis_index("head") * out_width, out_width, 1)
    decoded = (residual + summed).astype(jnp.bfloat16).reshape(1, steps, samples, out_width)
    return (decoded, kv_cache)


def solution(mesh):
    return jax.shard_map(
        local,
        mesh=mesh,
        in_specs=(
            P(None, "ctx", "head"),
            P(),
            P(),
            P("ctx", None, None, None),
            P(),
            P(),
            P(),
            P("ctx", "head"),
            P(None, None, "head"),
            P("head", "ctx"),
        ),
        out_specs=(P("ctx", None, None, "head"), P("ctx", None, None, "head")),
        check_vma=False,
    )
```

```python
import functools

import jax
import jax.numpy as jnp
from jax import lax
from jax.experimental import pallas as pl
from jax.experimental.pallas import tpu as pltpu
from jax.sharding import PartitionSpec as P

EPS = 1e-06
THETA = 1000000.0
CHUNKS = 2


def rotary(vector, position):
    half_size = vector.shape[-1] // 2
    frequency = THETA ** (-jnp.arange(half_size, dtype=jnp.float32) * 2.0 / vector.shape[-1])
    angle = position[..., None] * frequency
    cosine = jnp.cos(angle)
    sine = jnp.sin(angle)
    first = vector[..., :half_size]
    second = vector[..., half_size:]
    return jnp.concatenate([first * cosine - second * sine, second * cosine + first * sine], -1)


def head_norm(vector, gain):
    return vector * lax.rsqrt(jnp.mean(vector * vector, -1, keepdims=True) + EPS) * gain


def attend(queries, prefix_keys, prefix_values, new_keys, new_values, length, samples):
    total_rows = queries.shape[0]
    prefix_scores = jnp.einsum(
        "rkgd,lkd->kgrl", queries, prefix_keys, preferred_element_type=jnp.float32
    )
    suffix_scores = jnp.einsum(
        "rkgd,ukd->kgru", queries, new_keys, preferred_element_type=jnp.float32
    )
    live = jnp.arange(prefix_keys.shape[0]) < length
    prefix_scores = jnp.where(live, prefix_scores, -1e30)
    row_index = jnp.arange(total_rows)
    same_sample = row_index[:, None] % samples == row_index[None, :] % samples
    earlier = row_index[None, :] // samples <= row_index[:, None] // samples
    suffix_scores = jnp.where(same_sample & earlier, suffix_scores, -1e30)
    top = jnp.maximum(
        jnp.max(prefix_scores, -1, keepdims=True), jnp.max(suffix_scores, -1, keepdims=True)
    )
    prefix_exp = jnp.exp(prefix_scores - top)
    suffix_exp = jnp.exp(suffix_scores - top)
    total = jnp.sum(prefix_exp, -1, keepdims=True) + jnp.sum(suffix_exp, -1, keepdims=True)
    prefix_weight = (prefix_exp / total).astype(jnp.bfloat16)
    suffix_weight = (suffix_exp / total).astype(jnp.bfloat16)
    result = jnp.einsum(
        "kgrl,lkd->rkgd", prefix_weight, prefix_values, preferred_element_type=jnp.float32
    )
    result = result + jnp.einsum(
        "kgru,ukd->rkgd", suffix_weight, new_values, preferred_element_type=jnp.float32
    )
    return result.reshape(total_rows, -1).astype(jnp.bfloat16)


def project_kernel(
    ctx_size, head_size, attended_ref, w_ref, out_ref,
    gathered, partial, landed, gather_send, gather_recv, part_send, part_recv, own_sem,
):
    ctx = lax.axis_index("ctx")
    head = lax.axis_index("head")
    per = ctx_size // head_size
    owner = ctx // per
    rank = ctx % per
    is_owner = owner == head
    mesh_id = pl.DeviceIdType.MESH

    barrier = pltpu.get_barrier_semaphore()
    for k in range(1, ctx_size):
        source = lax.rem(ctx - k + ctx_size, ctx_size)
        pl.semaphore_signal(barrier, inc=1, device_id=(source, head), device_id_type=mesh_id)
    for h in range(head_size):
        for r in range(per):
            source = head * per + r

            @pl.when(jnp.logical_or(source != ctx, h != head))
            def _():
                pl.semaphore_signal(barrier, inc=1, device_id=(source, h), device_id_type=mesh_id)

    @pl.when(is_owner)
    def _():
        pl.semaphore_wait(barrier, 2 * ctx_size - 2)

    @pl.when(jnp.logical_not(is_owner))
    def _():
        pl.semaphore_wait(barrier, 2 * ctx_size - 1)

    def gather_copy(k):
        target = lax.rem(ctx + k, ctx_size)
        return pltpu.make_async_remote_copy(
            src_ref=attended_ref, dst_ref=gathered.at[k],
            send_sem=gather_send.at[k], recv_sem=gather_recv.at[k],
            device_id=(target, head), device_id_type=mesh_id,
        )

    def part_copy(k):
        target = lax.rem(ctx - k + ctx_size, ctx_size)
        slot = head * per + rank
        return pltpu.make_async_remote_copy(
            src_ref=partial.at[k], dst_ref=landed.at[slot],
            send_sem=part_send.at[k], recv_sem=part_recv.at[slot],
            device_id=(target, owner), device_id_type=mesh_id,
        )

    def own_copy():
        return pltpu.make_async_copy(partial.at[0], landed.at[head * per + rank], own_sem)

    for k in range(1, ctx_size):
        gather_copy(k).start()
    gathered[0] = attended_ref[...]
    rows, depth = attended_ref.shape
    width = w_ref.shape[1]
    half = ctx_size // 2
    for part in range(2):
        first = part * half
        for k in range(max(first, 1), first + half):
            gather_copy(k).wait_recv()
        block = gathered[first : first + half].reshape(half * rows, depth)
        product = jnp.dot(block, w_ref[...], preferred_element_type=jnp.float32)
        partial[first : first + half] = product.reshape(half, rows, width)
        for k in range(first, first + half):
            if k:
                part_copy(k).start()
            else:

                @pl.when(is_owner)
                def _():
                    own_copy().start()

                @pl.when(jnp.logical_not(is_owner))
                def _():
                    part_copy(0).start()

    for k in range(1, ctx_size):
        gather_copy(k).wait_send()
    for r in range(per):
        source = head * per + r
        for h in range(head_size):
            mine = jnp.logical_and(source == ctx, h == head)
            slot = h * per + r

            @pl.when(mine)
            def _():
                own_copy().wait()

            @pl.when(jnp.logical_not(mine))
            def _():
                pltpu.make_async_remote_copy(
                    src_ref=partial.at[0], dst_ref=landed.at[slot],
                    send_sem=part_send.at[0], recv_sem=part_recv.at[slot],
                    device_id=(source, h), device_id_type=mesh_id,
                ).wait_recv()

        total = landed[r]
        for h in range(1, head_size):
            total = total + landed[h * per + r]
        out_ref[:, r * width : (r + 1) * width] = total
    for k in range(ctx_size):
        if k:
            part_copy(k).wait_send()
        else:

            @pl.when(jnp.logical_not(is_owner))
            def _():
                part_copy(0).wait_send()


def project(attended, w_o):
    ctx_size = lax.axis_size("ctx")
    head_size = lax.axis_size("head")
    per = ctx_size // head_size
    rows, depth = attended.shape
    width = w_o.shape[1]
    return pl.pallas_call(
        functools.partial(project_kernel, ctx_size, head_size),
        out_shape=jax.ShapeDtypeStruct((rows, per * width), jnp.float32),
        in_specs=[pl.BlockSpec(memory_space=pltpu.VMEM)] * 2,
        out_specs=pl.BlockSpec(memory_space=pltpu.VMEM),
        scratch_shapes=[
            pltpu.VMEM((ctx_size, rows, depth), jnp.bfloat16),
            pltpu.VMEM((ctx_size, rows, width), jnp.float32),
            pltpu.VMEM((head_size * per, rows, width), jnp.float32),
            pltpu.SemaphoreType.DMA((ctx_size,)),
            pltpu.SemaphoreType.DMA((ctx_size,)),
            pltpu.SemaphoreType.DMA((ctx_size,)),
            pltpu.SemaphoreType.DMA((head_size * per,)),
            pltpu.SemaphoreType.DMA,
        ],
        compiler_params=pltpu.CompilerParams(
            collective_id=0, has_side_effects=True, vmem_limit_bytes=32 * 1024 * 1024
        ),
        cost_estimate=pl.CostEstimate(
            flops=2 * ctx_size * rows * depth * width,
            bytes_accessed=2 * (depth * width + ctx_size * rows * depth),
            transcendentals=0,
        ),
    )(attended, w_o)


def local(
    prompt_hidden,
    prompt_lengths,
    group_prompt,
    sample_hidden,
    norm_gain,
    q_gain,
    k_gain,
    w_q,
    w_kv,
    w_o,
):
    prompts, slab, part_width = prompt_hidden.shape
    model_width = norm_gain.shape[0]
    head_dim = q_gain.shape[0]
    kv_width = w_kv.shape[2]
    kv_local = kv_width // head_dim
    q_width = w_q.shape[1]
    q_local = q_width // head_dim
    group_size = q_local // kv_local
    ctx_index = lax.axis_index("ctx")
    ctx_size = lax.axis_size("ctx")
    flat_weights = w_kv.reshape(model_width, 2 * kv_width)
    steps = sample_hidden.shape[1]
    samples = sample_hidden.shape[2]
    token_rows = steps * samples
    wide = sample_hidden.reshape(token_rows, model_width).astype(jnp.float32)
    token_inverse = lax.rsqrt(jnp.mean(wide * wide, -1) + EPS)[:, None]
    token_scaled = (wide * norm_gain).astype(jnp.bfloat16)
    row_depth = w_q.shape[0]
    by_feature = token_scaled.reshape(token_rows, ctx_size, row_depth).transpose(1, 0, 2)
    all_tokens = lax.all_to_all(by_feature, "ctx", split_axis=0, concat_axis=0, tiled=True)
    query_part = jnp.dot(
        all_tokens.reshape(ctx_size * token_rows, row_depth), w_q, preferred_element_type=jnp.float32
    ).reshape(ctx_size, token_rows, q_width)
    query_part = lax.all_to_all(query_part, "ctx", split_axis=0, concat_axis=0, tiled=True)
    queries = jnp.sum(query_part, 0) * token_inverse

    chunk_rows = slab // CHUNKS
    exchange = functools.partial(
        lax.all_to_all, axis_name="ctx", split_axis=0, concat_axis=0, tiled=True
    )
    cache_chunks = []
    for chunk in range(CHUNKS):
        hidden = lax.slice_in_dim(prompt_hidden, chunk * chunk_rows, (chunk + 1) * chunk_rows, axis=1)
        piece = lax.all_gather(hidden, "head", axis=2, tiled=True)
        if cache_chunks:
            piece, cache_chunks[-1] = lax.optimization_barrier((piece, exchange(ordered)))
        wide_piece = piece.astype(jnp.float32).reshape(prompts * chunk_rows, model_width)
        scaled_piece = (wide_piece * norm_gain).astype(jnp.bfloat16)
        running_sum = jnp.dot(scaled_piece, flat_weights, preferred_element_type=jnp.float32)
        squares = jnp.sum(wide_piece * wide_piece, -1)
        prefill_inverse = lax.rsqrt(squares / model_width + EPS)[:, None]
        raw = (running_sum * prefill_inverse).reshape(prompts, chunk_rows, 2, kv_local, head_dim)
        positions = (
            ctx_index * slab + chunk * chunk_rows + jnp.arange(chunk_rows, dtype=jnp.int32)
        ).astype(jnp.float32)
        prompt_keys = rotary(head_norm(raw[:, :, 0], k_gain), positions[None, :, None])
        cache_local = jnp.stack([prompt_keys, raw[:, :, 1]], 2).astype(jnp.bfloat16)
        cache_local = cache_local.reshape(prompts, chunk_rows, 2, kv_width)
        ordered = jnp.take(cache_local, group_prompt, axis=0)
        cache_chunks.append(None)
    cache_chunks[-1] = exchange(ordered)
    kv_cache = jnp.stack(cache_chunks, 1).reshape(1, ctx_size * slab, 2, kv_width)
    length = jnp.take(prompt_lengths, jnp.take(group_prompt, ctx_index))
    fresh = jnp.dot(token_scaled, flat_weights, preferred_element_type=jnp.float32) * token_inverse
    fresh = fresh.reshape(token_rows, 2, kv_local, head_dim)
    row_position = jnp.repeat(length + jnp.arange(steps, dtype=jnp.int32), samples).astype(
        jnp.float32
    )
    queries = rotary(
        head_norm(queries.reshape(token_rows, q_local, head_dim), q_gain), row_position[:, None]
    )
    queries = (queries * head_dim ** (-0.5)).astype(jnp.bfloat16)
    queries = queries.reshape(token_rows, kv_local, group_size, head_dim)
    new_keys = rotary(head_norm(fresh[:, 0], k_gain), row_position[:, None]).astype(jnp.bfloat16)
    new_values = fresh[:, 1].astype(jnp.bfloat16)
    prefix_keys = kv_cache[0, :, 0].reshape(-1, kv_local, head_dim)
    prefix_values = kv_cache[0, :, 1].reshape(-1, kv_local, head_dim)
    attended = attend(queries, prefix_keys, prefix_values, new_keys, new_values, length, samples)
    summed = project(attended, w_o)
    out_width = summed.shape[1]
    residual = lax.dynamic_slice_in_dim(wide, lax.axis_index("head") * out_width, out_width, 1)
    decoded = (residual + summed).astype(jnp.bfloat16).reshape(1, steps, samples, out_width)
    return (decoded, kv_cache)


def solution(mesh):
    return jax.shard_map(
        local,
        mesh=mesh,
        in_specs=(
            P(None, "ctx", "head"),
            P(),
            P(),
            P("ctx", None, None, None),
            P(),
            P(),
            P(),
            P("ctx", "head"),
            P(None, None, "head"),
            P("head", "ctx"),
        ),
        out_specs=(P("ctx", None, None, "head"), P("ctx", None, None, "head")),
        check_vma=False,
    )
```
